32 devices in a mesh: fsdp: 2 (over x), dp: 16 (over z, y, core).
Axes of the slice: x: 2, y: 2, z: 4, core: 2. Of those that a mesh axis runs over, the one named last changes fastest.
Arguments:
- hidden_in: bfloat16 [64, 512, 768], P(('fsdp', 'dp')), may hold values from -6 to 6
- lengths: int32 [64], P(('fsdp', 'dp')), may hold values from 1 to 512, 17920 in all
- query_w: bfloat16 [768, 768], P('fsdp'), may hold values from -0.21875 to 0.21875
- key_w: bfloat16 [768, 768], P('fsdp'), may hold values from -0.21875 to 0.21875
- value_w: bfloat16 [768, 768], P('fsdp'), may hold values from -0.21875 to 0.21875
- out_w: bfloat16 [768, 768], P('fsdp'), may hold values from -1.75 to 1.75
- query_b: bfloat16 [768], P('fsdp'), may hold values from -3 to 3
- value_b: bfloat16 [768], P('fsdp'), may hold values from -3 to 3
- out_b: bfloat16 [768], P('fsdp'), may hold values from -3 to 3
- gain_one: bfloat16 [768], P('fsdp'), may hold values from 0.5 to 1.5
- shift_one: bfloat16 [768], P('fsdp'), may hold values from -3 to 3
- up_w: bfloat16 [768, 3072], P('fsdp'), may hold values from -0.21875 to 0.21875
- up_b: bfloat16 [3072], P('fsdp'), may hold values from -3 to 3
- down_w: bfloat16 [3072, 768], P('fsdp'), may hold values from -0.109375 to 0.109375
- down_b: bfloat16 [768], P('fsdp'), may hold values from -3 to 3
- gain_two: bfloat16 [768], P('fsdp'), may hold values from 0.5 to 1.5
- shift_two: bfloat16 [768], P('fsdp'), may hold values from -3 to 3
- cotangent: bfloat16 [64, 512, 768], P(('fsdp', 'dp')), may hold values from -6 to 6
Outputs:
- block_out: bfloat16 [64, 512, 768], P(('fsdp', 'dp'))
- grad_in: float32 [64, 512, 768], P(('fsdp', 'dp'))
- grad_query_w: float32 [768, 768], P('fsdp')
- grad_key_w: float32 [768, 768], P('fsdp')
- grad_value_w: float32 [768, 768], P('fsdp')
- grad_out_w: float32 [768, 768], P('fsdp')
- grad_query_b: float32 [768], P('fsdp')
- grad_value_b: float32 [768], P('fsdp')
- grad_out_b: float32 [768], P('fsdp')
- grad_gain_one: float32 [768], P('fsdp')
- grad_shift_one: float32 [768], P('fsdp')
- grad_up_w: float32 [768, 3072], P('fsdp')
- grad_up_b: float32 [3072], P('fsdp')
- grad_down_w: float32 [3072, 768], P('fsdp')
- grad_down_b: float32 [768], P('fsdp')
- grad_gain_two: float32 [768], P('fsdp')
- grad_shift_two: float32 [768], P('fsdp')
The draws below stay inside these ranges and needn't reach their ends.
Inputs may be any that keep to these rules, and one draw needn't show every extreme that they name: `lengths`: the longest sequence of the whole batch has exactly 512 real tokens.
All inputs are finite; a program needn't handle non-finite values. No bound on the sum of `lengths` on one device may be relied on, other than what follows from the above.
Results may differ from the reference program's by a relative error of at most 0.014.
Values may be sent and summed in bfloat16 or wider, within the bound.
A program may use at most 192 MiB of HBM per device.

```python
import math
import jax
import jax.numpy as jnp
import numpy as np
from jax import lax

D = 768
HEADS = 12
FF = 3072
LEN = 512
SEQS = 64


def steps_of(stream_key, dims, cuts, smallest, high):
    factor_of, own = 1.0, jax.random.fold_in(stream_key, 6)
    for position, parts in cuts:
        steps = jnp.exp(jax.random.uniform(jax.random.fold_in(own, position), (parts,), jnp.float32, smallest / len(cuts), high / len(cuts)))
        factor_of = factor_of * jnp.repeat(steps, dims[position] // parts).reshape([-1 if axis == position else 1 for axis in range(len(dims))])
    return factor_of


def length_profile(count, total, reach, slope):
    weights = [(1 << 20) // math.isqrt(grade ** slope) + 1 for grade in range(2, count + 1)]
    surplus, counts = total - reach - (count - 1), [1] * (count - 1)
    while surplus > 0:
        free = [i for i in range(count - 1) if counts[i] < reach]
        whole, budget = sum([weights[i] for i in free]), surplus
        for i in free:
            addition = min(reach - counts[i], max(1, budget * weights[i] // whole), surplus)
            counts[i] = counts[i] + addition
            surplus = surplus - addition
    return np.array([reach] + counts)


def ragged(stream_key, amount, total, bound, skew):
    if amount == 2:
        one = jax.random.randint(stream_key, (), max(1, total - bound), min(bound, total - 1) + 1)
        return jnp.stack([one, total - one])
    sizes = jnp.asarray(length_profile(amount, total, bound, skew), jnp.int32)
    couples = (amount - 1) // 2
    source_of, receiver = sizes[1:1 + 2 * couples:2], sizes[2:2 + 2 * couples:2]
    margin = jnp.minimum(source_of - 1, bound - receiver)
    shifted = jax.random.randint(jax.random.fold_in(stream_key, 1), (couples,), 0, 1 << 20) % (margin + 1)
    sizes = sizes.at[1:1 + 2 * couples:2].set(source_of - shifted).at[2:2 + 2 * couples:2].set(receiver + shifted)
    return sizes[jax.random.permutation(jax.random.fold_in(stream_key, 2), amount)]


def scatter_about(rng, shape, scale, bound, shards=(), held_as=jnp.bfloat16):
    values = scale * jax.random.normal(rng, shape, jnp.float32)
    if shards:
        values = values * steps_of(rng, shape, shards, -0.22, 0.18)
    return jnp.clip(values, -bound, bound).astype(held_as)


def setup_inputs(seed: int = 0) -> dict:
    streams_of = jax.random.split(jax.random.key(seed), 19)
    return {
        "hidden_in": scatter_about(streams_of[0], (SEQS, LEN, D), 1.0, 6.0, ((0, 32),)),
        "lengths": ragged(streams_of[1], SEQS, SEQS * LEN * 35 // 64, LEN, 1).astype(jnp.int32),
        "query_w": scatter_about(streams_of[2], (D, D), D ** -0.5, 0.21875, ((0, 2),)),
        "key_w": scatter_about(streams_of[3], (D, D), D ** -0.5, 0.21875, ((0, 2),)),
        "value_w": scatter_about(streams_of[4], (D, D), D ** -0.5, 0.21875, ((0, 2),)),
        "out_w": scatter_about(streams_of[5], (D, D), (D * 8 // LEN) ** -0.5, 1.75, ((0, 2),)),
        "query_b": scatter_about(streams_of[6], (D,), 0.5, 3.0, ((0, 2),)),
        "value_b": scatter_about(streams_of[7], (D,), 0.5, 3.0, ((0, 2),)),
        "out_b": scatter_about(streams_of[8], (D,), 0.5, 3.0, ((0, 2),)),
        "gain_one": jnp.clip(1.0 + 0.1 * jax.random.normal(streams_of[9], (D,), jnp.float32), 0.5, 1.5).astype(jnp.bfloat16),
        "shift_one": scatter_about(streams_of[10], (D,), 0.5, 3.0, ((0, 2),)),
        "up_w": scatter_about(streams_of[11], (D, FF), D ** -0.5, 0.21875, ((0, 2),)),
        "up_b": scatter_about(streams_of[12], (FF,), 0.5, 3.0, ((0, 2),)),
        "down_w": scatter_about(streams_of[13], (FF, D), FF ** -0.5, 0.109375, ((0, 2),)),
        "down_b": scatter_about(streams_of[14], (D,), 0.5, 3.0, ((0, 2),)),
        "gain_two": jnp.clip(1.0 + 0.1 * jax.random.normal(streams_of[15], (D,), jnp.float32), 0.5, 1.5).astype(jnp.bfloat16),
        "shift_two": scatter_about(streams_of[16], (D,), 0.5, 3.0, ((0, 2),)),
        "cotangent": scatter_about(streams_of[17], (SEQS, LEN, D), 1.0, 6.0, ((0, 32),)),
    }


@jax.custom_vjp
def low(v):
    return lax.optimization_barrier(v.astype(jnp.bfloat16)).astype(jnp.float32)

@jax.custom_vjp
def low_back(v):
    return v

def low_keep(v):
    return (low(v), None)

def low_pass(kept, grad):
    return (grad,)

def back_keep(v):
    return (v, None)

def back_low(kept, grad):
    return (low(grad),)
low.defvjp(low_keep, low_pass)
low_back.defvjp(back_keep, back_low)
precision_highest = lax.Precision.HIGHEST
norm_eps = 1e-12
mask_fill = -1e+30

def product_high(left, right):
    return jnp.dot(left, right, precision=precision_highest, preferred_element_type=jnp.float32)

def layer_norm(summed, gain, shift):
    average = lax.optimization_barrier(jnp.mean(summed, axis=-1, keepdims=True))
    centred = summed - average
    inverse = lax.rsqrt(lax.optimization_barrier(jnp.mean(centred * centred, axis=-1, keepdims=True)) + norm_eps)
    return centred * inverse * gain + shift

def attend(query_vectors, key_vectors, value_vectors, length):
    score_scale = 1.0 / math.sqrt(query_vectors.shape[-1])
    unmasked_score_matrix = jnp.einsum('gyx,uyx->ygu', query_vectors, key_vectors, precision=precision_highest)
    scores = low_back(unmasked_score_matrix * score_scale)
    allowed = jnp.arange(key_vectors.shape[0], dtype=jnp.int32) < length
    scores = jnp.where(allowed[None, None, :], scores, mask_fill)
    attention_probs = low(jax.nn.softmax(scores, axis=-1))
    return jnp.einsum('kuo,okq->ukq', attention_probs, value_vectors, precision=precision_highest)

def attend_item(item):
    return jax.checkpoint(attend)(item[0], item[1], item[2], item[3])

def forward(params, block, seq_lengths):
    query_w, key_w, value_w, out_w, query_b, value_b, out_b, gain_one, shift_one, up_w, up_b, down_w, down_b, gain_two, shift_two = params
    count, seq_len, width = block.shape
    flat = block.reshape(count * seq_len, width)
    query_vectors = low(low_back(product_high(flat, query_w) + query_b))
    key_vectors = low(low_back(product_high(flat, key_w)))
    value_vectors = low(low_back(product_high(flat, value_w) + value_b))
    shaped = (count, seq_len, HEADS, width // HEADS)
    mixed = lax.map(attend_item, (query_vectors.reshape(shaped), key_vectors.reshape(shaped), value_vectors.reshape(shaped), seq_lengths))
    mixed = low(low_back(mixed.reshape(count * seq_len, width)))
    branch = low_back(product_high(mixed, out_w) + out_b)
    first = layer_norm(flat + branch, gain_one, shift_one)
    inner = low_back(product_high(low(first), up_w) + up_b)
    hidden_low = low(jax.nn.gelu(inner, approximate=False))
    second = low_back(product_high(hidden_low, down_w) + down_b)
    return layer_norm(first + second, gain_two, shift_two).reshape(block.shape)

def reference(hidden_in, lengths, query_w, key_w, value_w, out_w, query_b, value_b, out_b, gain_one, shift_one, up_w, up_b, down_w, down_b, gain_two, shift_two, cotangent):
    params = tuple((param.astype(jnp.float32) for param in (query_w, key_w, value_w, out_w, query_b, value_b, out_b, gain_one, shift_one, up_w, up_b, down_w, down_b, gain_two, shift_two)))
    per_group = math.gcd(SEQS, max(1, 4096 // LEN))
    groups = SEQS // per_group
    blocks = hidden_in.astype(jnp.float32).reshape(groups, per_group, LEN, D)
    group_lengths = lengths.reshape(groups, per_group)
    group_cot = cotangent.astype(jnp.float32).reshape(groups, per_group, LEN, D)

    def one_group(totals, item):
        block, seq_lengths, cot_block = item
        result, pullback = jax.vjp(lambda param_set, rows_in: forward(param_set, rows_in, seq_lengths), params, block)
        positions = jnp.arange(LEN, dtype=jnp.int32)
        valid = (positions[None, :] < seq_lengths[:, None]).astype(jnp.float32)
        grad_params, grad_block = pullback(cot_block * valid[:, :, None])
        totals = jax.tree.map(lambda total, grad: total + grad, totals, grad_params)
        return (totals, (result.astype(jnp.bfloat16), grad_block))
    zeros = jax.tree.map(jnp.zeros_like, params)
    totals, (results, grads_in) = lax.scan(one_group, zeros, (blocks, group_lengths, group_cot))
    block_out = results.reshape(SEQS, LEN, D)
    grad_in = grads_in.reshape(SEQS, LEN, D)
    return (block_out, grad_in, totals[0], totals[1], totals[2], totals[3], totals[4], totals[5], totals[6], totals[7], totals[8], totals[9], totals[10], totals[11], totals[12], totals[13], totals[14])
```

```python
import math

import jax
import jax.numpy as jnp
from jax import lax
from jax.sharding import PartitionSpec as P

HEADS = 12


norm_eps = 1e-12
mask_fill = -1e30


def product(left, right):
    return jnp.dot(left, right, preferred_element_type=jnp.float32)


def trans_left(left, right):
    return lax.dot_general(
        left, right, (((0,), (0,)), ((), ())), preferred_element_type=jnp.float32
    )


def trans_right(left, right):
    return lax.dot_general(
        left, right, (((1,), (1,)), ((), ())), preferred_element_type=jnp.float32
    )


def normalize(summed):
    average = jnp.mean(summed, axis=-1, keepdims=True)
    centred = summed - average
    inverse = lax.rsqrt(jnp.mean(centred * centred, axis=-1, keepdims=True) + norm_eps)
    return (centred * inverse, inverse)


def norm_back(grad_normed, normed, inverse):
    first_mean = jnp.mean(grad_normed, axis=-1, keepdims=True)
    cross_mean = jnp.mean(grad_normed * normed, axis=-1, keepdims=True)
    return inverse * (grad_normed - first_mean - normed * cross_mean)


def masked_scores(query_vectors, key_vectors, length):
    score_scale = 1.0 / math.sqrt(query_vectors.shape[-1])
    unmasked_score_matrix = (
        jnp.einsum("gyx,uyx->ygu", query_vectors, key_vectors, preferred_element_type=jnp.float32)
        * score_scale
    )
    allowed = jnp.arange(key_vectors.shape[0], dtype=jnp.int32) < length
    return (jnp.where(allowed[None, None, :], unmasked_score_matrix, mask_fill), score_scale)


def attend_one(item):
    query_vectors, key_vectors, value_vectors, length = item
    scores, score_scale = masked_scores(query_vectors, key_vectors, length)
    precision_highest = jnp.max(scores, axis=-1, keepdims=True)
    exponent = jnp.exp(scores - precision_highest)
    totals = jnp.sum(exponent, axis=-1, keepdims=True)
    attention_probs = exponent / totals
    log_total = precision_highest + jnp.log(totals)
    mixed = jnp.einsum(
        "kuo,okq->ukq",
        attention_probs.astype(jnp.bfloat16),
        value_vectors,
        preferred_element_type=jnp.float32,
    )
    return (mixed.astype(jnp.bfloat16), log_total)


def attend_back(item):
    query_vectors, key_vectors, value_vectors, length, log_total, gradient_context_rows = item
    scores, score_scale = masked_scores(query_vectors, key_vectors, length)
    attention_probs = jnp.exp(scores - log_total)
    attention_probs_reduced = attention_probs.astype(jnp.bfloat16)
    grad_attention = jnp.einsum(
        "gyx,uyx->ygu", gradient_context_rows, value_vectors, preferred_element_type=jnp.float32
    )
    weighted = jnp.sum(attention_probs * grad_attention, axis=-1, keepdims=True)
    gradient_score_matrix = (attention_probs * (grad_attention - weighted)).astype(jnp.bfloat16)
    grad_query = (
        jnp.einsum(
            "kuo,okq->ukq", gradient_score_matrix, key_vectors, preferred_element_type=jnp.float32
        )
        * score_scale
    )
    grad_keys = (
        jnp.einsum(
            "ygu,gyp->uyp", gradient_score_matrix, query_vectors, preferred_element_type=jnp.float32
        )
        * score_scale
    )
    grad_values = jnp.einsum(
        "ygu,gyp->uyp",
        attention_probs_reduced,
        gradient_context_rows,
        preferred_element_type=jnp.float32,
    )
    return (
        grad_query.astype(jnp.bfloat16),
        grad_keys.astype(jnp.bfloat16),
        grad_values.astype(jnp.bfloat16),
    )


def core_pairs():
    count = lax.axis_size("dp")
    return [(index, index ^ 1) for index in range(count)]


def same_core_groups():
    count = lax.axis_size("dp")
    return [list(range(core, count, 2)) for core in range(2)]


def own_core():
    return lax.rem(lax.axis_index("dp"), 2)


def join_cores(mine, theirs):
    lower = own_core() == 0
    return jnp.stack([jnp.where(lower, mine, theirs), jnp.where(lower, theirs, mine)], axis=-3)


def gather_weight(shard):
    rows, columns = shard.shape
    half = rows // 2
    mine = lax.dynamic_slice_in_dim(shard, own_core() * half, half, axis=0)
    mine = lax.all_gather(mine, "fsdp", axis=0, tiled=False)
    theirs = lax.ppermute(mine, "dp", core_pairs())
    return join_cores(mine, theirs).reshape(-1, columns)


def gather_vectors(vectors):
    whole = lax.all_gather(jnp.concatenate(vectors), "fsdp", axis=0, tiled=False)
    pieces, start = [], 0
    for vector in vectors:
        size = vector.shape[0]
        pieces.append(whole[:, start : start + size].reshape(-1).astype(jnp.float32))
        start += size
    return pieces


def core_sum(grad):
    groups = lax.axis_size("fsdp")
    rows, columns = grad.shape
    cut = grad.astype(jnp.bfloat16).reshape(groups, 2, rows // (2 * groups), columns)
    core = own_core()
    kept = lax.dynamic_index_in_dim(cut, core, axis=1, keepdims=False)
    sent = lax.dynamic_index_in_dim(cut, 1 - core, axis=1, keepdims=False)
    return (
        kept.astype(jnp.float32) + lax.ppermute(sent, "dp", core_pairs()).astype(jnp.float32)
    ).astype(jnp.bfloat16)


def scatter_weight(grad):
    return lax.psum_scatter(core_sum(grad), "fsdp", scatter_dimension=0, tiled=False)


def sum_replicas(parts):
    return lax.psum(parts, "dp", axis_index_groups=same_core_groups())


def both_cores(part):
    theirs = lax.ppermute(part, "dp", core_pairs())
    return join_cores(part, theirs).reshape(-1, part.shape[-1]).astype(jnp.float32)


def sum_vectors(grads):
    groups = lax.axis_size("fsdp")
    packed = jnp.concatenate([grad.reshape(groups, -1) for grad in grads], axis=1)
    packed = lax.psum(packed, ("fsdp", "dp"))
    mine = lax.dynamic_index_in_dim(packed, lax.axis_index("fsdp"), axis=0, keepdims=False)
    pieces, start = [], 0
    for grad in grads:
        size = grad.shape[0] // groups
        pieces.append(mine[start : start + size])
        start += size
    return pieces


def gelu_pair(inner):
    bell = jnp.exp(-0.5 * inner * inner)
    size = jnp.abs(inner) * (1.0 / math.sqrt(2.0))
    step = 1.0 / (1.0 + 0.3275911 * size)
    poly = step * (
        0.254829592
        + step * (-0.284496736 + step * (1.421413741 + step * (-1.453152027 + step * 1.061405429)))
    )
    tail = 0.5 * poly * bell
    share = jnp.where(inner < 0, tail, 1.0 - tail)
    slope = share + inner * bell * (1.0 / math.sqrt(2.0 * math.pi))
    return (inner * share).astype(jnp.bfloat16), slope.astype(jnp.bfloat16)


def shards(
    hidden_in,
    lengths,
    query_w,
    key_w,
    value_w,
    out_w,
    query_b,
    value_b,
    out_b,
    gain_one,
    shift_one,
    up_w,
    up_b,
    down_w,
    down_b,
    gain_two,
    shift_two,
    cotangent,
):
    seq_count, seq_len, width = hidden_in.shape
    token_rows = seq_count * seq_len
    heads_shape = (seq_count, seq_len, HEADS, width // HEADS)
    rows_in = hidden_in.reshape(token_rows, width)
    full_qkv = gather_weight(jnp.concatenate([query_w, key_w, value_w], axis=1))
    (
        full_query_b,
        full_value_b,
        full_out_b,
        full_gain_one,
        full_shift_one,
        full_up_b,
        full_down_b,
        full_gain_two,
        full_shift_two,
    ) = gather_vectors(
        [query_b, value_b, out_b, gain_one, shift_one, up_b, down_b, gain_two, shift_two]
    )
    full_out = gather_weight(out_w)
    full_up = gather_weight(up_w)
    full_down = gather_weight(down_w)
    qkv_bias = jnp.concatenate([full_query_b, jnp.zeros_like(full_query_b), full_value_b])
    qkv = (product(rows_in, full_qkv) + qkv_bias).astype(jnp.bfloat16)
    query_vectors, key_vectors, value_vectors = (
        part.reshape(heads_shape) for part in jnp.split(qkv, 3, axis=1)
    )
    mixed, log_total = lax.map(attend_one, (query_vectors, key_vectors, value_vectors, lengths))
    mixed_flat = mixed.reshape(token_rows, width)
    branch = product(mixed_flat, full_out) + full_out_b
    normed_one, inverse_one = normalize(rows_in.astype(jnp.float32) + branch)
    first = normed_one * full_gain_one + full_shift_one
    first_low = first.astype(jnp.bfloat16)
    inner = product(first_low, full_up) + full_up_b
    hidden_low, slope_low = gelu_pair(inner)
    second = product(hidden_low, full_down) + full_down_b
    normed_two, inverse_two = normalize(first + second)
    block_out = (
        (normed_two * full_gain_two + full_shift_two).astype(jnp.bfloat16).reshape(hidden_in.shape)
    )
    positions = jnp.arange(seq_len, dtype=jnp.int32)
    valid = (positions[None, :] < lengths[:, None]).astype(jnp.float32).reshape(token_rows, 1)
    grad_top = cotangent.reshape(token_rows, width).astype(jnp.float32) * valid
    grad_gain_two = jnp.sum(grad_top * normed_two, axis=0)
    grad_shift_two = jnp.sum(grad_top, axis=0)
    grad_sum_two = norm_back(grad_top * full_gain_two, normed_two, inverse_two)
    grad_second = grad_sum_two.astype(jnp.bfloat16)
    part_down = scatter_weight(trans_left(hidden_low, grad_second))
    grad_down_b = jnp.sum(grad_second.astype(jnp.float32), axis=0)
    grad_hidden = trans_right(grad_second, full_down)
    grad_inner = (grad_hidden * slope_low.astype(jnp.float32)).astype(jnp.bfloat16)
    part_up = scatter_weight(trans_left(first_low, grad_inner))
    grad_up_b = jnp.sum(grad_inner.astype(jnp.float32), axis=0)
    part_up, part_down = sum_replicas((part_up, part_down))
    grad_first = grad_sum_two + trans_right(grad_inner, full_up)
    grad_gain_one = jnp.sum(grad_first * normed_one, axis=0)
    grad_shift_one = jnp.sum(grad_first, axis=0)
    grad_sum_one = norm_back(grad_first * full_gain_one, normed_one, inverse_one)
    grad_branch = grad_sum_one.astype(jnp.bfloat16)
    part_out = scatter_weight(trans_left(mixed_flat, grad_branch))
    grad_out_b = jnp.sum(grad_branch.astype(jnp.float32), axis=0)
    grad_mixed = trans_right(grad_branch, full_out).astype(jnp.bfloat16)
    grad_query, grad_keys, grad_values = lax.map(
        attend_back,
        (
            query_vectors,
            key_vectors,
            value_vectors,
            lengths,
            log_total,
            grad_mixed.reshape(heads_shape),
        ),
    )
    grad_qkv = jnp.concatenate(
        [part.reshape(token_rows, width) for part in (grad_query, grad_keys, grad_values)], axis=1
    )
    grad_qkv_b = jnp.sum(grad_qkv.astype(jnp.float32), axis=0)
    part_qkv = scatter_weight(trans_left(rows_in, grad_qkv))
    grad_in = grad_sum_one + trans_right(grad_qkv, full_qkv)
    (
        own_query_b,
        own_value_b,
        own_out_b,
        own_gain_one,
        own_shift_one,
        own_up_b,
        own_down_b,
        own_gain_two,
        own_shift_two,
    ) = sum_vectors(
        [
            grad_qkv_b[:width],
            grad_qkv_b[2 * width :],
            grad_out_b,
            grad_gain_one,
            grad_shift_one,
            grad_up_b,
            grad_down_b,
            grad_gain_two,
            grad_shift_two,
        ]
    )
    part_out, part_qkv, part_up, part_down = lax.optimization_barrier(
        (part_out, part_qkv, part_up, part_down)
    )
    part_out, part_qkv = sum_replicas((part_out, part_qkv))
    own_up_w, own_down_w, own_out_w, own_qkv_w = (
        both_cores(part) for part in (part_up, part_down, part_out, part_qkv)
    )
    own_query_w, own_key_w, own_value_w = jnp.split(own_qkv_w, 3, axis=1)
    return (
        block_out,
        grad_in.reshape(hidden_in.shape),
        own_query_w,
        own_key_w,
        own_value_w,
        own_out_w,
        own_query_b,
        own_value_b,
        own_out_b,
        own_gain_one,
        own_shift_one,
        own_up_w,
        own_up_b,
        own_down_w,
        own_down_b,
        own_gain_two,
        own_shift_two,
    )


def solution(mesh):
    in_specs = (
        P(("fsdp", "dp"), None, None),
        P(("fsdp", "dp")),
        P("fsdp", None),
        P("fsdp", None),
        P("fsdp", None),
        P("fsdp", None),
        P("fsdp"),
        P("fsdp"),
        P("fsdp"),
        P("fsdp"),
        P("fsdp"),
        P("fsdp", None),
        P("fsdp"),
        P("fsdp", None),
        P("fsdp"),
        P("fsdp"),
        P("fsdp"),
        P(("fsdp", "dp"), None, None),
    )
    out_specs = (
        P(("fsdp", "dp"), None, None),
        P(("fsdp", "dp"), None, None),
        P("fsdp", None),
        P("fsdp", None),
        P("fsdp", None),
        P("fsdp", None),
        P("fsdp"),
        P("fsdp"),
        P("fsdp"),
        P("fsdp"),
        P("fsdp"),
        P("fsdp", None),
        P("fsdp"),
        P("fsdp", None),
        P("fsdp"),
        P("fsdp"),
        P("fsdp"),
    )
    return jax.shard_map(shards, mesh=mesh, in_specs=in_specs, out_specs=out_specs, check_vma=False)
```

```python
import math

import jax
import jax.numpy as jnp
from jax import lax
from jax.sharding import PartitionSpec as P

HEADS = 12


norm_eps = 1e-12
mask_fill = -1e30


def product(left, right):
    return jnp.dot(left, right, preferred_element_type=jnp.float32)


def trans_left(left, right):
    return lax.dot_general(
        left, right, (((0,), (0,)), ((), ())), preferred_element_type=jnp.float32
    )


def trans_right(left, right):
    return lax.dot_general(
        left, right, (((1,), (1,)), ((), ())), preferred_element_type=jnp.float32
    )


def normalize(summed):
    average = jnp.mean(summed, axis=-1, keepdims=True)
    centred = summed - average
    inverse = lax.rsqrt(jnp.mean(centred * centred, axis=-1, keepdims=True) + norm_eps)
    return (centred * inverse, inverse)


def norm_back(grad_normed, normed, inverse):
    first_mean = jnp.mean(grad_normed, axis=-1, keepdims=True)
    cross_mean = jnp.mean(grad_normed * normed, axis=-1, keepdims=True)
    return inverse * (grad_normed - first_mean - normed * cross_mean)


def masked_scores(query_vectors, key_vectors, length):
    score_scale = 1.0 / math.sqrt(query_vectors.shape[-1])
    unmasked_score_matrix = (
        jnp.einsum("gyx,uyx->ygu", query_vectors, key_vectors, preferred_element_type=jnp.float32)
        * score_scale
    )
    allowed = jnp.arange(key_vectors.shape[0], dtype=jnp.int32) < length
    return (jnp.where(allowed[None, None, :], unmasked_score_matrix, mask_fill), score_scale)


def attend_one(item):
    query_vectors, key_vectors, value_vectors, length = item
    scores, score_scale = masked_scores(query_vectors, key_vectors, length)
    precision_highest = jnp.max(scores, axis=-1, keepdims=True)
    exponent = jnp.exp(scores - precision_highest)
    totals = jnp.sum(exponent, axis=-1, keepdims=True)
    attention_probs = exponent / totals
    log_total = precision_highest + jnp.log(totals)
    mixed = jnp.einsum(
        "kuo,okq->ukq",
        attention_probs.astype(jnp.bfloat16),
        value_vectors,
        preferred_element_type=jnp.float32,
    )
    return (mixed.astype(jnp.bfloat16), log_total)


def attend_back(item):
    query_vectors, key_vectors, value_vectors, length, log_total, gradient_context_rows = item
    scores, score_scale = masked_scores(query_vectors, key_vectors, length)
    attention_probs = jnp.exp(scores - log_total)
    attention_probs_reduced = attention_probs.astype(jnp.bfloat16)
    grad_attention = jnp.einsum(
        "gyx,uyx->ygu", gradient_context_rows, value_vectors, preferred_element_type=jnp.float32
    )
    weighted = jnp.sum(attention_probs * grad_attention, axis=-1, keepdims=True)
    gradient_score_matrix = (attention_probs * (grad_attention - weighted)).astype(jnp.bfloat16)
    grad_query = (
        jnp.einsum(
            "kuo,okq->ukq", gradient_score_matrix, key_vectors, preferred_element_type=jnp.float32
        )
        * score_scale
    )
    grad_keys = (
        jnp.einsum(
            "ygu,gyp->uyp", gradient_score_matrix, query_vectors, preferred_element_type=jnp.float32
        )
        * score_scale
    )
    grad_values = jnp.einsum(
        "ygu,gyp->uyp",
        attention_probs_reduced,
        gradient_context_rows,
        preferred_element_type=jnp.float32,
    )
    return (
        grad_query.astype(jnp.bfloat16),
        grad_keys.astype(jnp.bfloat16),
        grad_values.astype(jnp.bfloat16),
    )


def core_pairs():
    count = lax.axis_size("dp")
    return [(index, index ^ 1) for index in range(count)]


def same_core_groups():
    count = lax.axis_size("dp")
    return [list(range(core, count, 2)) for core in range(2)]


def own_core():
    return lax.rem(lax.axis_index("dp"), 2)


def join_cores(mine, theirs):
    lower = own_core() == 0
    return jnp.stack([jnp.where(lower, mine, theirs), jnp.where(lower, theirs, mine)], axis=-3)


def row_pairs(distance):
    return [(index, index ^ distance) for index in range(lax.axis_size("fsdp"))]


def gather_halves(shard):
    half = shard.shape[0] // 2
    mine = lax.dynamic_slice_in_dim(shard, own_core() * half, half, axis=0)[None]
    distance = 1
    while distance < lax.axis_size("fsdp"):
        theirs = lax.ppermute(mine, "fsdp", row_pairs(distance))
        lower = lax.rem(lax.axis_index("fsdp") // distance, 2) == 0
        mine = jnp.concatenate(
            [jnp.where(lower, mine, theirs), jnp.where(lower, theirs, mine)], axis=0
        )
        distance *= 2
    return mine, lax.ppermute(mine, "dp", core_pairs())


def join_weight(halves):
    return join_cores(*halves).reshape(-1, halves[0].shape[-1])


def gather_vectors(vectors):
    whole = lax.all_gather(jnp.concatenate(vectors), "fsdp", axis=0, tiled=False)
    pieces, start = [], 0
    for vector in vectors:
        size = vector.shape[0]
        pieces.append(whole[:, start : start + size].reshape(-1).astype(jnp.float32))
        start += size
    return pieces


def core_sum(grad):
    groups = lax.axis_size("fsdp")
    rows, columns = grad.shape
    cut = grad.astype(jnp.bfloat16).reshape(groups, 2, rows // (2 * groups), columns)
    core = own_core()
    kept = lax.dynamic_index_in_dim(cut, core, axis=1, keepdims=False)
    sent = lax.dynamic_index_in_dim(cut, 1 - core, axis=1, keepdims=False)
    return (
        kept.astype(jnp.float32) + lax.ppermute(sent, "dp", core_pairs()).astype(jnp.float32)
    ).astype(jnp.bfloat16)


def scatter_weight(part):
    distance = lax.axis_size("fsdp") // 2
    while distance >= 1:
        bit = lax.rem(lax.axis_index("fsdp") // distance, 2)
        cut = part.reshape(2, distance, *part.shape[1:])
        kept = lax.dynamic_index_in_dim(cut, bit, axis=0, keepdims=False)
        sent = lax.dynamic_index_in_dim(cut, 1 - bit, axis=0, keepdims=False)
        theirs = lax.ppermute(sent, "fsdp", row_pairs(distance))
        part = (kept.astype(jnp.float32) + theirs.astype(jnp.float32)).astype(jnp.bfloat16)
        distance //= 2
    return part[0]


def sum_replicas(parts):
    return lax.psum(parts, "dp", axis_index_groups=same_core_groups())


def both_cores(part):
    theirs = lax.ppermute(part, "dp", core_pairs())
    return join_cores(part, theirs).reshape(-1, part.shape[-1]).astype(jnp.float32)


def pack_vectors(grads):
    groups = lax.axis_size("fsdp")
    packed = jnp.concatenate([grad.reshape(groups, -1) for grad in grads], axis=1)
    return scatter_weight(core_sum(packed.reshape(2 * groups, -1)))


def unpack_vectors(mine, grads):
    pieces, start = [], 0
    for grad in grads:
        size = grad.shape[0] // lax.axis_size("fsdp")
        pieces.append(mine[start : start + size])
        start += size
    return pieces


def gelu_pair(inner):
    bell = jnp.exp(-0.5 * inner * inner)
    size = jnp.abs(inner) * (1.0 / math.sqrt(2.0))
    step = 1.0 / (1.0 + 0.3275911 * size)
    poly = step * (
        0.254829592
        + step * (-0.284496736 + step * (1.421413741 + step * (-1.453152027 + step * 1.061405429)))
    )
    tail = 0.5 * poly * bell
    share = jnp.where(inner < 0, tail, 1.0 - tail)
    slope = share + inner * bell * (1.0 / math.sqrt(2.0 * math.pi))
    return (inner * share).astype(jnp.bfloat16), slope.astype(jnp.bfloat16)


def shards(
    hidden_in,
    lengths,
    query_w,
    key_w,
    value_w,
    out_w,
    query_b,
    value_b,
    out_b,
    gain_one,
    shift_one,
    up_w,
    up_b,
    down_w,
    down_b,
    gain_two,
    shift_two,
    cotangent,
):
    seq_count, seq_len, width = hidden_in.shape
    token_rows = seq_count * seq_len
    heads_shape = (seq_count, seq_len, HEADS, width // HEADS)
    rows_in = hidden_in.reshape(token_rows, width)
    qkv_halves = gather_halves(jnp.concatenate([query_w, key_w, value_w], axis=1))
    full_qkv = join_weight(qkv_halves)
    (
        full_query_b,
        full_value_b,
        full_out_b,
        full_gain_one,
        full_shift_one,
        full_up_b,
        full_down_b,
        full_gain_two,
        full_shift_two,
    ) = gather_vectors(
        [query_b, value_b, out_b, gain_one, shift_one, up_b, down_b, gain_two, shift_two]
    )
    _, up_shard, down_shard, out_shard = lax.optimization_barrier(
        (qkv_halves[0], up_w, down_w, out_w)
    )
    later_halves = tuple(gather_halves(shard) for shard in (out_shard, up_shard, down_shard))
    qkv_bias = jnp.concatenate([full_query_b, jnp.zeros_like(full_query_b), full_value_b])
    qkv = (product(rows_in, full_qkv) + qkv_bias).astype(jnp.bfloat16)
    query_vectors, key_vectors, value_vectors = (
        part.reshape(heads_shape) for part in jnp.split(qkv, 3, axis=1)
    )
    forward = [
        attend_one((query_vectors[seq], key_vectors[seq], value_vectors[seq], lengths[seq]))
        for seq in range(seq_count)
    ]
    mixed_flat = jnp.concatenate([mixed for mixed, _ in forward]).reshape(token_rows, width)
    mixed_flat, later_halves = lax.optimization_barrier((mixed_flat, later_halves))
    full_out, full_up, full_down = (join_weight(halves) for halves in later_halves)
    branch = product(mixed_flat, full_out) + full_out_b
    normed_one, inverse_one = normalize(rows_in.astype(jnp.float32) + branch)
    first = normed_one * full_gain_one + full_shift_one
    first_low = first.astype(jnp.bfloat16)
    inner = product(first_low, full_up) + full_up_b
    hidden_low, slope_low = gelu_pair(inner)
    second = product(hidden_low, full_down) + full_down_b
    normed_two, inverse_two = normalize(first + second)
    block_out = (
        (normed_two * full_gain_two + full_shift_two).astype(jnp.bfloat16).reshape(hidden_in.shape)
    )
    positions = jnp.arange(seq_len, dtype=jnp.int32)
    valid = (positions[None, :] < lengths[:, None]).astype(jnp.float32).reshape(token_rows, 1)
    grad_top = cotangent.reshape(token_rows, width).astype(jnp.float32) * valid
    grad_gain_two = jnp.sum(grad_top * normed_two, axis=0)
    grad_shift_two = jnp.sum(grad_top, axis=0)
    grad_sum_two = norm_back(grad_top * full_gain_two, normed_two, inverse_two)
    grad_second = grad_sum_two.astype(jnp.bfloat16)
    core_down = core_sum(trans_left(hidden_low, grad_second))
    grad_down_b = jnp.sum(grad_second.astype(jnp.float32), axis=0)
    grad_hidden = trans_right(grad_second, full_down)
    grad_inner = (grad_hidden * slope_low.astype(jnp.float32)).astype(jnp.bfloat16)
    grad_inner, core_down = lax.optimization_barrier((grad_inner, core_down))
    part_down = scatter_weight(core_down)
    core_up = core_sum(trans_left(first_low, grad_inner))
    grad_up_b = jnp.sum(grad_inner.astype(jnp.float32), axis=0)
    grad_first = grad_sum_two + trans_right(grad_inner, full_up)
    grad_first, part_down = lax.optimization_barrier((grad_first, part_down))
    part_down = sum_replicas(part_down)
    grad_gain_one = jnp.sum(grad_first * normed_one, axis=0)
    grad_shift_one = jnp.sum(grad_first, axis=0)
    grad_sum_one = norm_back(grad_first * full_gain_one, normed_one, inverse_one)
    grad_branch = grad_sum_one.astype(jnp.bfloat16)
    core_out = core_sum(trans_left(mixed_flat, grad_branch))
    grad_out_b = jnp.sum(grad_branch.astype(jnp.float32), axis=0)
    grad_mixed = trans_right(grad_branch, full_out).astype(jnp.bfloat16)
    grad_mixed, core_up = lax.optimization_barrier((grad_mixed, core_up))
    part_up = scatter_weight(core_up)
    grad_context = grad_mixed.reshape(heads_shape)
    backward = []
    for seq in range(seq_count):
        context_rows = grad_context[seq]
        if seq == 1:
            context_rows, backward, part_up = lax.optimization_barrier(
                (context_rows, backward, part_up)
            )
        backward.append(
            attend_back(
                (
                    query_vectors[seq],
                    key_vectors[seq],
                    value_vectors[seq],
                    lengths[seq],
                    forward[seq][1],
                    context_rows,
                )
            )
        )
    part_out = scatter_weight(core_out)
    grad_qkv = jnp.concatenate(
        [
            jnp.concatenate([part.reshape(seq_len, width) for part in parts], axis=1)
            for parts in backward
        ]
    )
    grad_qkv, part_out, part_up, part_down = lax.optimization_barrier(
        (grad_qkv, part_out, part_up, part_down)
    )
    part_up = sum_replicas(part_up)
    grad_qkv_b = jnp.sum(grad_qkv.astype(jnp.float32), axis=0)
    part_qkv = core_sum(trans_left(rows_in, grad_qkv))
    grad_in = grad_sum_one + trans_right(grad_qkv, full_qkv)
    vector_grads = [
        grad_qkv_b[:width],
        grad_qkv_b[2 * width :],
        grad_out_b,
        grad_gain_one,
        grad_shift_one,
        grad_up_b,
        grad_down_b,
        grad_gain_two,
        grad_shift_two,
    ]
    part_vectors = pack_vectors(vector_grads)
    part_out, part_qkv, part_up, part_down = lax.optimization_barrier(
        (part_out, part_qkv, part_up, part_down)
    )
    part_out, part_qkv, part_vectors = sum_replicas(
        (part_out, scatter_weight(part_qkv), part_vectors)
    )
    (
        own_query_b,
        own_value_b,
        own_out_b,
        own_gain_one,
        own_shift_one,
        own_up_b,
        own_down_b,
        own_gain_two,
        own_shift_two,
    ) = unpack_vectors(both_cores(part_vectors).reshape(-1), vector_grads)
    own_up_w, own_down_w, own_out_w, own_qkv_w = (
        both_cores(part) for part in (part_up, part_down, part_out, part_qkv)
    )
    own_query_w, own_key_w, own_value_w = jnp.split(own_qkv_w, 3, axis=1)
    return (
        block_out,
        grad_in.reshape(hidden_in.shape),
        own_query_w,
        own_key_w,
        own_value_w,
        own_out_w,
        own_query_b,
        own_value_b,
        own_out_b,
        own_gain_one,
        own_shift_one,
        own_up_w,
        own_up_b,
        own_down_w,
        own_down_b,
        own_gain_two,
        own_shift_two,
    )


def solution(mesh):
    in_specs = (
        P(("fsdp", "dp"), None, None),
        P(("fsdp", "dp")),
        P("fsdp", None),
        P("fsdp", None),
        P("fsdp", None),
        P("fsdp", None),
        P("fsdp"),
        P("fsdp"),
        P("fsdp"),
        P("fsdp"),
        P("fsdp"),
        P("fsdp", None),
        P("fsdp"),
        P("fsdp", None),
        P("fsdp"),
        P("fsdp"),
        P("fsdp"),
        P(("fsdp", "dp"), None, None),
    )
    out_specs = (
        P(("fsdp", "dp"), None, None),
        P(("fsdp", "dp"), None, None),
        P("fsdp", None),
        P("fsdp", None),
        P("fsdp", None),
        P("fsdp", None),
        P("fsdp"),
        P("fsdp"),
        P("fsdp"),
        P("fsdp"),
        P("fsdp"),
        P("fsdp", None),
        P("fsdp"),
        P("fsdp", None),
        P("fsdp"),
        P("fsdp"),
        P("fsdp"),
    )
    return jax.shard_map(shards, mesh=mesh, in_specs=in_specs, out_specs=out_specs, check_vma=False)
```

```python
import math

import jax
import jax.numpy as jnp
from jax import lax
from jax.sharding import PartitionSpec as P

HEADS = 12


norm_eps = 1e-12
mask_fill = -1e30


def product(left, right):
    return jnp.dot(left, right, preferred_element_type=jnp.float32)


def trans_left(left, right):
    return lax.dot_general(
        left, right, (((0,), (0,)), ((), ())), preferred_element_type=jnp.float32
    )


def trans_right(left, right):
    return lax.dot_general(
        left, right, (((1,), (1,)), ((), ())), preferred_element_type=jnp.float32
    )


def normalize(summed):
    average = jnp.mean(summed, axis=-1, keepdims=True)
    centred = summed - average
    inverse = lax.rsqrt(jnp.mean(centred * centred, axis=-1, keepdims=True) + norm_eps)
    return (centred * inverse, inverse)


def norm_back(grad_normed, normed, inverse):
    first_mean = jnp.mean(grad_normed, axis=-1, keepdims=True)
    cross_mean = jnp.mean(grad_normed * normed, axis=-1, keepdims=True)
    return inverse * (grad_normed - first_mean - normed * cross_mean)


def masked_scores(query_vectors, key_vectors, length):
    score_scale = 1.0 / math.sqrt(query_vectors.shape[-1])
    unmasked_score_matrix = (
        jnp.einsum("gyx,uyx->ygu", query_vectors, key_vectors, preferred_element_type=jnp.float32)
        * score_scale
    )
    allowed = jnp.arange(key_vectors.shape[0], dtype=jnp.int32) < length
    return (jnp.where(allowed[None, None, :], unmasked_score_matrix, mask_fill), score_scale)


def attend_one(item):
    query_vectors, key_vectors, value_vectors, length = item
    scores, score_scale = masked_scores(query_vectors, key_vectors, length)
    precision_highest = jnp.max(scores, axis=-1, keepdims=True)
    exponent = jnp.exp(scores - precision_highest)
    totals = jnp.sum(exponent, axis=-1, keepdims=True)
    attention_probs = exponent / totals
    log_total = precision_highest + jnp.log(totals)
    mixed = jnp.einsum(
        "kuo,okq->ukq",
        attention_probs.astype(jnp.bfloat16),
        value_vectors,
        preferred_element_type=jnp.float32,
    )
    return (mixed.astype(jnp.bfloat16), log_total)


def attend_back(item):
    query_vectors, key_vectors, value_vectors, length, log_total, gradient_context_rows = item
    scores, score_scale = masked_scores(query_vectors, key_vectors, length)
    attention_probs = jnp.exp(scores - log_total)
    attention_probs_reduced = attention_probs.astype(jnp.bfloat16)
    grad_attention = jnp.einsum(
        "gyx,uyx->ygu", gradient_context_rows, value_vectors, preferred_element_type=jnp.float32
    )
    weighted = jnp.sum(attention_probs * grad_attention, axis=-1, keepdims=True)
    gradient_score_matrix = (attention_probs * (grad_attention - weighted)).astype(jnp.bfloat16)
    grad_query = (
        jnp.einsum(
            "kuo,okq->ukq", gradient_score_matrix, key_vectors, preferred_element_type=jnp.float32
        )
        * score_scale
    )
    grad_keys = (
        jnp.einsum(
            "ygu,gyp->uyp", gradient_score_matrix, query_vectors, preferred_element_type=jnp.float32
        )
        * score_scale
    )
    grad_values = jnp.einsum(
        "ygu,gyp->uyp",
        attention_probs_reduced,
        gradient_context_rows,
        preferred_element_type=jnp.float32,
    )
    return (
        grad_query.astype(jnp.bfloat16),
        grad_keys.astype(jnp.bfloat16),
        grad_values.astype(jnp.bfloat16),
    )


def core_pairs():
    count = lax.axis_size("dp")
    return [(index, index ^ 1) for index in range(count)]


def same_core_groups():
    count = lax.axis_size("dp")
    return [list(range(core, count, 2)) for core in range(2)]


def own_core():
    return lax.rem(lax.axis_index("dp"), 2)


def join_cores(mine, theirs):
    lower = own_core() == 0
    return jnp.stack([jnp.where(lower, mine, theirs), jnp.where(lower, theirs, mine)], axis=-3)


def row_pairs(distance):
    return [(index, index ^ distance) for index in range(lax.axis_size("fsdp"))]


def gather_halves(shard):
    half = shard.shape[0] // 2
    mine = lax.dynamic_slice_in_dim(shard, own_core() * half, half, axis=0)[None]
    distance = 1
    while distance < lax.axis_size("fsdp"):
        theirs = lax.ppermute(mine, "fsdp", row_pairs(distance))
        lower = lax.rem(lax.axis_index("fsdp") // distance, 2) == 0
        mine = jnp.concatenate(
            [jnp.where(lower, mine, theirs), jnp.where(lower, theirs, mine)], axis=0
        )
        distance *= 2
    return mine, lax.ppermute(mine, "dp", core_pairs())


def join_weight(halves):
    return join_cores(*halves).reshape(-1, halves[0].shape[-1])


def gather_vectors(vectors):
    whole = lax.all_gather(jnp.concatenate(vectors), "fsdp", axis=0, tiled=False)
    pieces, start = [], 0
    for vector in vectors:
        size = vector.shape[0]
        pieces.append(whole[:, start : start + size].reshape(-1).astype(jnp.float32))
        start += size
    return pieces


def core_sum(grad):
    groups = lax.axis_size("fsdp")
    rows, columns = grad.shape
    cut = grad.astype(jnp.bfloat16).reshape(groups, 2, rows // (2 * groups), columns)
    core = own_core()
    kept = lax.dynamic_index_in_dim(cut, core, axis=1, keepdims=False)
    sent = lax.dynamic_index_in_dim(cut, 1 - core, axis=1, keepdims=False)
    return (
        kept.astype(jnp.float32) + lax.ppermute(sent, "dp", core_pairs()).astype(jnp.float32)
    ).astype(jnp.bfloat16)


def scatter_weight(part):
    distance = lax.axis_size("fsdp") // 2
    while distance >= 1:
        bit = lax.rem(lax.axis_index("fsdp") // distance, 2)
        cut = part.reshape(2, distance, *part.shape[1:])
        kept = lax.dynamic_index_in_dim(cut, bit, axis=0, keepdims=False)
        sent = lax.dynamic_index_in_dim(cut, 1 - bit, axis=0, keepdims=False)
        theirs = lax.ppermute(sent, "fsdp", row_pairs(distance))
        part = (kept.astype(jnp.float32) + theirs.astype(jnp.float32)).astype(jnp.bfloat16)
        distance //= 2
    return part[0]


def sum_replicas(parts):
    return lax.psum(parts, "dp", axis_index_groups=same_core_groups())


def both_cores(part):
    theirs = lax.ppermute(part, "dp", core_pairs())
    return join_cores(part, theirs).reshape(-1, part.shape[-1]).astype(jnp.float32)


def pack_vectors(grads):
    groups = lax.axis_size("fsdp")
    packed = jnp.concatenate([grad.reshape(groups, -1) for grad in grads], axis=1)
    return scatter_weight(core_sum(packed.reshape(2 * groups, -1)))


def unpack_vectors(mine, grads):
    pieces, start = [], 0
    for grad in grads:
        size = grad.shape[0] // lax.axis_size("fsdp")
        pieces.append(mine[start : start + size])
        start += size
    return pieces


def gelu_pair(inner):
    bell = jnp.exp(-0.5 * inner * inner)
    size = jnp.abs(inner) * (1.0 / math.sqrt(2.0))
    step = 1.0 / (1.0 + 0.3275911 * size)
    poly = step * (
        0.254829592
        + step * (-0.284496736 + step * (1.421413741 + step * (-1.453152027 + step * 1.061405429)))
    )
    tail = 0.5 * poly * bell
    share = jnp.where(inner < 0, tail, 1.0 - tail)
    slope = share + inner * bell * (1.0 / math.sqrt(2.0 * math.pi))
    return (inner * share).astype(jnp.bfloat16), slope.astype(jnp.bfloat16)


def shards(
    hidden_in,
    lengths,
    query_w,
    key_w,
    value_w,
    out_w,
    query_b,
    value_b,
    out_b,
    gain_one,
    shift_one,
    up_w,
    up_b,
    down_w,
    down_b,
    gain_two,
    shift_two,
    cotangent,
):
    seq_count, seq_len, width = hidden_in.shape
    token_rows = seq_count * seq_len
    heads_shape = (seq_count, seq_len, HEADS, width // HEADS)
    rows_in = hidden_in.reshape(token_rows, width)
    qkv_halves = gather_halves(jnp.concatenate([query_w, key_w, value_w], axis=1))
    full_qkv = join_weight(qkv_halves)
    (
        full_query_b,
        full_value_b,
        full_out_b,
        full_gain_one,
        full_shift_one,
        full_up_b,
        full_down_b,
        full_gain_two,
        full_shift_two,
    ) = gather_vectors(
        [query_b, value_b, out_b, gain_one, shift_one, up_b, down_b, gain_two, shift_two]
    )
    _, up_shard, down_shard, out_shard = lax.optimization_barrier(
        (qkv_halves[0], up_w, down_w, out_w)
    )
    later_halves = tuple(gather_halves(shard) for shard in (out_shard, up_shard, down_shard))
    qkv_bias = jnp.concatenate([full_query_b, jnp.zeros_like(full_query_b), full_value_b])
    qkv = (product(rows_in, full_qkv) + qkv_bias).astype(jnp.bfloat16)
    query_vectors, key_vectors, value_vectors = (
        part.reshape(heads_shape) for part in jnp.split(qkv, 3, axis=1)
    )
    forward = [
        attend_one((query_vectors[seq], key_vectors[seq], value_vectors[seq], lengths[seq]))
        for seq in range(seq_count)
    ]
    mixed_flat = jnp.concatenate([mixed for mixed, _ in forward]).reshape(token_rows, width)
    mixed_flat, later_halves = lax.optimization_barrier((mixed_flat, later_halves))
    full_out, full_up, full_down = (join_weight(halves) for halves in later_halves)
    branch = product(mixed_flat, full_out) + full_out_b
    normed_one, inverse_one = normalize(rows_in.astype(jnp.float32) + branch)
    first = normed_one * full_gain_one + full_shift_one
    first_low = first.astype(jnp.bfloat16)
    inner = product(first_low, full_up) + full_up_b
    hidden_low, slope_low = gelu_pair(inner)
    second = product(hidden_low, full_down) + full_down_b
    normed_two, inverse_two = normalize(first + second)
    block_out = (
        (normed_two * full_gain_two + full_shift_two).astype(jnp.bfloat16).reshape(hidden_in.shape)
    )
    positions = jnp.arange(seq_len, dtype=jnp.int32)
    valid = (positions[None, :] < lengths[:, None]).astype(jnp.float32).reshape(token_rows, 1)
    grad_top = cotangent.reshape(token_rows, width).astype(jnp.float32) * valid
    grad_gain_two = jnp.sum(grad_top * normed_two, axis=0)
    grad_shift_two = jnp.sum(grad_top, axis=0)
    grad_sum_two = norm_back(grad_top * full_gain_two, normed_two, inverse_two)
    grad_second = grad_sum_two.astype(jnp.bfloat16)
    core_down = core_sum(trans_left(hidden_low, grad_second))
    grad_down_b = jnp.sum(grad_second.astype(jnp.float32), axis=0)
    grad_hidden = trans_right(grad_second, full_down)
    grad_inner = (grad_hidden * slope_low.astype(jnp.float32)).astype(jnp.bfloat16)
    grad_inner, core_down = lax.optimization_barrier((grad_inner, core_down))
    part_down = scatter_weight(core_down)
    core_up = core_sum(trans_left(first_low, grad_inner))
    grad_up_b = jnp.sum(grad_inner.astype(jnp.float32), axis=0)
    grad_first = grad_sum_two + trans_right(grad_inner, full_up)
    grad_first, part_down = lax.optimization_barrier((grad_first, part_down))
    part_down = sum_replicas(part_down)
    grad_gain_one = jnp.sum(grad_first * normed_one, axis=0)
    grad_shift_one = jnp.sum(grad_first, axis=0)
    grad_sum_one = norm_back(grad_first * full_gain_one, normed_one, inverse_one)
    grad_branch = grad_sum_one.astype(jnp.bfloat16)
    core_out = core_sum(trans_left(mixed_flat, grad_branch))
    grad_out_b = jnp.sum(grad_branch.astype(jnp.float32), axis=0)
    grad_mixed = trans_right(grad_branch, full_out).astype(jnp.bfloat16)
    grad_mixed, core_up = lax.optimization_barrier((grad_mixed, core_up))
    part_up = scatter_weight(core_up)
    grad_context = grad_mixed.reshape(heads_shape)
    backward = []
    for seq in range(seq_count):
        context_rows = grad_context[seq]
        if seq == 1:
            context_rows, backward, part_up = lax.optimization_barrier(
                (context_rows, backward, part_up)
            )
        backward.append(
            attend_back(
                (
                    query_vectors[seq],
                    key_vectors[seq],
                    value_vectors[seq],
                    lengths[seq],
                    forward[seq][1],
                    context_rows,
                )
            )
        )
    part_out = scatter_weight(core_out)
    grad_parts = lax.optimization_barrier(
        tuple(
            jnp.concatenate([part.reshape(seq_len, width) for part in parts])
            for parts in zip(*backward)
        )
    )
    grad_qkv = jnp.concatenate(grad_parts, axis=1)
    part_up, part_down = lax.optimization_barrier((part_up, part_down))
    part_up = sum_replicas(part_up)
    grad_qkv, part_out, part_down = lax.optimization_barrier((grad_qkv, part_out, part_down))
    grad_qkv_b = jnp.sum(grad_qkv.astype(jnp.float32), axis=0)
    part_qkv = core_sum(trans_left(rows_in, grad_qkv))
    grad_in = grad_sum_one + trans_right(grad_qkv, full_qkv)
    vector_grads = [
        grad_qkv_b[:width],
        grad_qkv_b[2 * width :],
        grad_out_b,
        grad_gain_one,
        grad_shift_one,
        grad_up_b,
        grad_down_b,
        grad_gain_two,
        grad_shift_two,
    ]
    part_vectors = pack_vectors(vector_grads)
    part_qkv = scatter_weight(part_qkv)
    part_out, part_qkv, part_up, part_down = lax.optimization_barrier(
        (part_out, part_qkv, part_up, part_down)
    )
    out_rows, vector_size = part_out.shape[0], part_vectors.size
    padded = jnp.pad(part_vectors.reshape(-1), (0, -vector_size % width)).reshape(-1, width)
    joined, part_qkv = sum_replicas((jnp.concatenate([part_out, padded]), part_qkv))
    part_out = joined[:out_rows]
    part_vectors = joined[out_rows:].reshape(1, -1)[:, :vector_size]
    (
        own_query_b,
        own_value_b,
        own_out_b,
        own_gain_one,
        own_shift_one,
        own_up_b,
        own_down_b,
        own_gain_two,
        own_shift_two,
    ) = unpack_vectors(both_cores(part_vectors).reshape(-1), vector_grads)
    own_up_w, own_down_w, own_out_w, own_qkv_w = (
        both_cores(part) for part in (part_up, part_down, part_out, part_qkv)
    )
    own_query_w, own_key_w, own_value_w = jnp.split(own_qkv_w, 3, axis=1)
    return (
        block_out,
        grad_in.reshape(hidden_in.shape),
        own_query_w,
        own_key_w,
        own_value_w,
        own_out_w,
        own_query_b,
        own_value_b,
        own_out_b,
        own_gain_one,
        own_shift_one,
        own_up_w,
        own_up_b,
        own_down_w,
        own_down_b,
        own_gain_two,
        own_shift_two,
    )


def solution(mesh):
    in_specs = (
        P(("fsdp", "dp"), None, None),
        P(("fsdp", "dp")),
        P("fsdp", None),
        P("fsdp", None),
        P("fsdp", None),
        P("fsdp", None),
        P("fsdp"),
        P("fsdp"),
        P("fsdp"),
        P("fsdp"),
        P("fsdp"),
        P("fsdp", None),
        P("fsdp"),
        P("fsdp", None),
        P("fsdp"),
        P("fsdp"),
        P("fsdp"),
        P(("fsdp", "dp"), None, None),
    )
    out_specs = (
        P(("fsdp", "dp"), None, None),
        P(("fsdp", "dp"), None, None),
        P("fsdp", None),
        P("fsdp", None),
        P("fsdp", None),
        P("fsdp", None),
        P("fsdp"),
        P("fsdp"),
        P("fsdp"),
        P("fsdp"),
        P("fsdp"),
        P("fsdp", None),
        P("fsdp"),
        P("fsdp", None),
        P("fsdp"),
        P("fsdp"),
        P("fsdp"),
    )
    return jax.shard_map(shards, mesh=mesh, in_specs=in_specs, out_specs=out_specs, check_vma=False)
```
